256 devices in a mesh: noise: 8 (over x, core), dp: 32 (over y, z).
Axes of the slice: x: 4, y: 4, z: 8, core: 2. Of those that a mesh axis runs over, the one named last changes fastest.
Arguments:
- noise_latents: bfloat16 [8192, 1024], P('noise', 'dp'), may hold values from -8 to 8
- data_latents: bfloat16 [32768, 1024], P('dp', 'noise'), may hold values from -8 to 8
Outputs:
- targets: float32 [8192, 1024], P('noise', 'dp')
- row_potential: float32 [8192], P('noise')
- col_potential: float32 [32768], P('dp')
The draws below stay inside these ranges and needn't reach their ends.
All inputs are finite; a program needn't handle non-finite values.
Results may differ from the reference program's by a relative error of at most 0.0027.
Values may be sent and summed in bfloat16 or wider, within the bound.
A program may use at most 64 MiB of HBM per device.

```python
import jax
import jax.numpy as jnp

D = 1024
ITERS = 3
NOISE_ROWS = 8192
DATA_ROWS = 32768


def draw_noise_latents(key, part):
    key = jax.random.fold_in(key, 11)
    key_values = jax.random.fold_in(key, 1)
    values = jax.random.truncated_normal(key_values, -6.0, 6.0, (NOISE_ROWS, D), jnp.float32)
    return values.astype(jnp.bfloat16)


def draw_data_latents(key, part):
    key = jax.random.fold_in(key, 23)
    key_values = jax.random.fold_in(key, 1)
    values = jax.random.truncated_normal(key_values, -6.0, 6.0, (DATA_ROWS, D), jnp.float32)
    return values.astype(jnp.bfloat16)


def setup_inputs(seed: int = 0) -> dict:
    key_of = jax.random.split(jax.random.key(seed), 3)
    noise_latents = draw_noise_latents(jax.random.fold_in(key_of[2], 71), 0)
    data_latents = draw_data_latents(jax.random.fold_in(key_of[2], 71), 0)
    return {"noise_latents": noise_latents, "data_latents": data_latents}


epsilon_value = 0.05


def reference(noise_latents, data_latents):
    noise_norms = jnp.sum(jnp.square(noise_latents.astype(jnp.float32)), axis=1)
    data_norms = jnp.sum(jnp.square(data_latents.astype(jnp.float32)), axis=1)
    inner = jnp.dot(noise_latents, data_latents.T, preferred_element_type=jnp.float32)
    distance = (noise_norms[:, None] + data_norms[None, :] - 2.0 * inner) / D
    log_rows = jnp.log(jnp.float32(NOISE_ROWS))
    log_cols = jnp.log(jnp.float32(DATA_ROWS))

    def row_update(col_potential):
        logits = (col_potential[None, :] - distance) / epsilon_value
        return -epsilon_value * (jax.nn.logsumexp(logits, axis=1) - log_cols)

    col_potential = jnp.zeros((DATA_ROWS,), jnp.float32)
    for number in range(ITERS):
        row_potential = row_update(col_potential)
        logits = (row_potential[:, None] - distance) / epsilon_value
        col_potential = -epsilon_value * (jax.nn.logsumexp(logits, axis=0) - log_rows)
    row_potential = row_update(col_potential)
    weights = (jnp.exp((row_potential[:, None] + col_potential[None, :] - distance) / epsilon_value) / DATA_ROWS).astype(jnp.bfloat16)
    targets = jnp.dot(weights, data_latents, preferred_element_type=jnp.float32)
    return targets, row_potential, col_potential
```

```python
import math

import jax
import jax.numpy as jnp
from jax import lax
from jax.experimental import pallas as pl
from jax.experimental.pallas import tpu as pltpu
from jax.sharding import PartitionSpec as P

D = 1024
ITERS = 3
EPS = 0.05
ROWS = 1024
COLS = 1024
NX, NY, NZ = 4, 4, 8
WIDTH = D // (NY * NZ)
DEPTH = D // (2 * NX)
F32, BF16 = jnp.float32, jnp.bfloat16
MESH = pl.DeviceIdType.MESH

LOG2E = math.log2(math.e)
TO_LOGIT = 2.0 * LOG2E / (D * EPS)
NORM_LOGIT = LOG2E / (D * EPS)
TO_POTENTIAL = EPS / LOG2E

GATHER_ZY = 768
SUM_ZY = 256


def hops(by):
    dy, dz = by
    return min(dy, NY - dy) + min(dz, NZ - dz)


DP_PEERS = sorted(
    ((dy, dz) for dy in range(NY) for dz in range(NZ) if dy or dz), key=lambda by: -hops(by)
)
NOISE_PEERS = [(2, 1), (2, 0), (1, 1), (3, 1), (1, 0), (3, 0), (0, 1)]
Z_NEAR = [1, 7, 2, 6, 3, 5, 4]
Z_FAR = [4, 3, 5, 2, 6, 1, 7]
Y_FAR = [2, 1, 3]
Y_NEAR = [1, 3, 2]


def rows_at(start, size):
    return pl.ds(pl.multiple_of(start, size), size)


def diagonal():
    sub = lax.broadcasted_iota(jnp.int32, (8, 128), 0)
    lane = lax.broadcasted_iota(jnp.int32, (8, 128), 1)
    return lane - sub


def spread(packed, wide):
    for a in range(8):
        wide[pl.ds(128 * a, 128), :] = jnp.broadcast_to(packed[a : a + 1, :], (128, 128)).T


def row_logsum(logit, wide, out, weights=None):
    def first(t, acc):
        r = rows_at(8 * t, 8)
        g = wide[r, :]
        return tuple(jnp.maximum(acc[c], logit[r, 128 * c : 128 * c + 128] + g) for c in range(8))

    low = tuple(jnp.full((8, 128), -jnp.inf, F32) for _ in range(8))
    acc = lax.fori_loop(0, COLS // 8, first, low, unroll=8)
    top = [jnp.broadcast_to(jnp.max(a, axis=0, keepdims=True), (8, 128)) for a in acc]
    zero = tuple(jnp.zeros((8, 128), F32) for _ in range(8))

    def second(t, acc):
        r = rows_at(8 * t, 8)
        g = wide[r, :]
        return tuple(
            acc[c] + jnp.exp2(logit[r, 128 * c : 128 * c + 128] + g - top[c]) for c in range(8)
        )

    def second_kept(t, acc):
        r = rows_at(16 * t, 16)
        g = wide[r, :]
        sums = []
        for c in range(8):
            both = jnp.concatenate([top[c], top[c]], axis=0)
            e = jnp.exp2(logit[r, 128 * c : 128 * c + 128] + g - both)
            weights[r, 128 * c : 128 * c + 128] = e.astype(BF16)
            sums.append(acc[c] + e[:8] + e[8:])
        return tuple(sums)

    if weights is None:
        acc = lax.fori_loop(0, COLS // 8, second, zero, unroll=8)
    else:
        acc = lax.fori_loop(0, COLS // 16, second_kept, zero, unroll=4)
    for c in range(8):
        out[c : c + 1, :] = top[c][:1] + jnp.log2(jnp.sum(acc[c], axis=0, keepdims=True))
    return top


def col_logsum(logit, packed, out):
    f = [jnp.broadcast_to(packed[c : c + 1, :], (8, 128)) for c in range(8)]
    off = diagonal()

    def block(a, _):
        acc = jnp.zeros((8, 128), F32)
        for b in range(16):
            r = rows_at(128 * a + 8 * b, 8)
            v = [logit[r, 128 * c : 128 * c + 128] + f[c] for c in range(8)]
            m = jnp.maximum(
                jnp.maximum(jnp.maximum(v[0], v[1]), jnp.maximum(v[2], v[3])),
                jnp.maximum(jnp.maximum(v[4], v[5]), jnp.maximum(v[6], v[7])),
            )
            m = jnp.max(m, axis=1, keepdims=True)
            e = [jnp.exp2(x - m) for x in v]
            s = ((e[0] + e[1]) + (e[2] + e[3])) + ((e[4] + e[5]) + (e[6] + e[7]))
            s = jnp.sum(s, axis=1, keepdims=True)
            acc = jnp.where(off == 8 * b, jnp.broadcast_to(m + jnp.log2(s), (8, 128)), acc)
        out[pl.ds(a, 1), :] = jnp.sum(acc, axis=0, keepdims=True)
        return 0

    lax.fori_loop(0, 8, block, 0)


def combine(parts, count):
    values = [parts[k] for k in range(count)]
    top = values[0]
    for v in values[1:]:
        top = jnp.maximum(top, v)
    total = jnp.exp2(values[0] - top)
    for v in values[1:]:
        total = total + jnp.exp2(v - top)
    return top + jnp.log2(total)


def norms(source, out):
    def step(t, acc):
        v = source[rows_at(16 * t, 16), :].astype(F32)
        v = v * v
        return acc + v[:8] + v[8:]

    acc = lax.fori_loop(0, D // 16, step, jnp.zeros((8, 1024), F32), unroll=2)
    s = jnp.sum(acc, axis=0, keepdims=True)
    for c in range(8):
        out[c : c + 1, :] = s[:, 128 * c : 128 * c + 128]


def kernel(
    noise_ref, data_ref, targets_ref, row_ref, col_ref,
    noise_full, data_full, data_t, logit, weights, partial, partial_half,
    wide, noise_norm, data_norm, f_packed, g_packed,
    row_parts, col_parts, sum_yz1, sum_yz2, sum_zy1, sum_zy2, send_yz2, send_zy2,
    own_sem, data_send, data_recv, pair_send, pair_recv,
    zy1_send, zy1_recv, zy2_send, zy2_recv, yz1_send, yz1_recv, yz2_send, yz2_recv,
    row_send, row_recv, col_send, col_recv,
    a1_send, a1_recv, a2_send, a2_recv, b1_send, b1_recv, b2_send, b2_recv,
):
    n = lax.axis_index("noise")
    k = lax.axis_index("dp")
    xs = [lax.rem(lax.div(n, 2) + d, NX) for d in range(NX)]
    cores = [lax.rem(n + d, 2) for d in range(2)]
    ys = [lax.rem(lax.div(k, NZ) + d, NY) for d in range(NY)]
    zs = [lax.rem(k + d, NZ) for d in range(NZ)]

    def dp_peer(dy, dz):
        return (n, ys[dy] * NZ + zs[dz])

    def noise_peer(dx, dc):
        return (xs[dx] * 2 + cores[dc], k)

    def remote(src, dst, send, recv, peer):
        copy = pltpu.make_async_remote_copy(
            src_ref=src, dst_ref=dst, send_sem=send, recv_sem=recv,
            device_id=peer, device_id_type=MESH,
        )
        copy.start()

    def wait_for(ref, sem):
        pltpu.make_async_copy(ref, ref, sem).wait()

    barrier = pltpu.get_barrier_semaphore()
    peers = [dp_peer(*by) for by in DP_PEERS] + [noise_peer(*by) for by in NOISE_PEERS]
    for peer in peers:
        pl.semaphore_signal(barrier, inc=1, device_id=peer, device_id_type=MESH)
    pl.semaphore_wait(barrier, len(peers))

    lanes_a, lanes_b = pl.ds(0, GATHER_ZY), pl.ds(GATHER_ZY, ROWS - GATHER_ZY)

    def noise_block(dy, dz, lanes):
        return noise_full.at[rows_at((ys[dy % NY] * NZ + zs[dz % NZ]) * WIDTH, WIDTH), lanes]

    def data_block(dx, dc):
        return data_full.at[:, rows_at((xs[dx % NX] * 2 + cores[dc]) * DEPTH, DEPTH)]

    own_noise = pltpu.make_async_copy(noise_ref, noise_block(0, 0, pl.ds(0, ROWS)), own_sem.at[0])
    own_noise.start()
    own_data = pltpu.make_async_copy(data_ref, data_block(0, 0), own_sem.at[1])
    own_data.start()
    for dz in Z_NEAR:
        remote(noise_ref.at[:, lanes_a], noise_block(0, 0, lanes_a), zy1_send, zy1_recv.at[dz], dp_peer(0, dz))
    for dy in Y_NEAR:
        remote(noise_ref.at[:, lanes_b], noise_block(0, 0, lanes_b), yz1_send, yz1_recv.at[dy], dp_peer(dy, 0))
    for dx in (1, 3, 2):
        remote(data_ref, data_block(0, 0), data_send, data_recv.at[dx], noise_peer(dx, 0))
    for dy in Y_FAR:
        remote(noise_ref.at[:, lanes_a], noise_block(0, 0, lanes_a), zy2_send, zy2_recv, dp_peer(dy, 0))
    for dz in Z_FAR:
        remote(noise_ref.at[:, lanes_b], noise_block(0, 0, lanes_b), yz2_send, yz2_recv, dp_peer(0, dz))
    remote(data_ref, data_block(0, 0), pair_send, pair_recv.at[0], noise_peer(0, 1))

    def forward_zy(dz):
        block = noise_block(0, -dz, lanes_a)
        wait_for(block, zy1_recv.at[dz])
        for dy in Y_FAR:
            remote(block, block, zy2_send, zy2_recv, dp_peer(dy, 0))

    def forward_yz(dy):
        block = noise_block(-dy, 0, lanes_b)
        wait_for(block, yz1_recv.at[dy])
        for dz in Z_FAR:
            remote(block, block, yz2_send, yz2_recv, dp_peer(0, dz))

    def forward_data(dx):
        block = data_block(-dx, 0)
        wait_for(block, data_recv.at[dx])
        remote(block, block, pair_send, pair_recv.at[dx], noise_peer(0, 1))

    forward_zy(1)
    forward_zy(7)
    forward_yz(1)
    forward_yz(3)
    forward_zy(2)
    forward_zy(6)
    forward_yz(2)
    forward_zy(3)
    forward_zy(5)
    forward_zy(4)
    forward_data(1)
    forward_data(3)
    forward_data(2)

    own_data.wait()
    for dx in range(NX):
        wait_for(data_block(-dx, 1), pair_recv.at[dx])

    def turn(t, _):
        r = rows_at(128 * t, 128)
        data_t[:, r] = data_full[r, :].T
        return 0

    lax.fori_loop(0, COLS // 128, turn, 0)
    norms(data_t, data_norm)
    g_packed[...] = data_norm[...] * (-NORM_LOGIT)
    spread(g_packed, wide)

    own_noise.wait()
    wait_for(noise_full.at[pl.ds(0, 24 * WIDTH), lanes_a], zy2_recv)
    wait_for(noise_full.at[pl.ds(0, 28 * WIDTH), lanes_b], yz2_recv)

    def product(t, _):
        r = rows_at(512 * t, 512)
        logit[r, :] = jnp.dot(data_full[r, :], noise_full[...], preferred_element_type=F32) * TO_LOGIT
        return 0

    lax.fori_loop(0, COLS // 512, product, 0)

    def send_row(t):
        own = row_parts.at[t, 31]
        for s, by in enumerate(DP_PEERS):
            remote(own, row_parts.at[t, s], row_send.at[t], row_recv.at[t], dp_peer(*by))

    def send_col(t):
        own = col_parts.at[t, 7]
        for s, by in enumerate(NOISE_PEERS):
            remote(own, col_parts.at[t, s], col_send.at[t], col_recv.at[t], noise_peer(*by))

    def iteration(t, _):
        row_logsum(logit, wide, row_parts.at[t, 31])
        send_row(t)
        wait_for(row_parts.at[t, pl.ds(0, 31)], row_recv.at[t])
        f_packed[...] = math.log2(COLS * NY * NZ) - combine(row_parts.at[t], 32)
        col_logsum(logit, f_packed, col_parts.at[t, 7])
        send_col(t)
        wait_for(col_parts.at[t, pl.ds(0, 7)], col_recv.at[t])
        g_packed[...] = math.log2(ROWS * NX * 2) - combine(col_parts.at[t], 8)
        spread(g_packed, wide)
        return 0

    lax.fori_loop(0, ITERS, iteration, 0)
    top = row_logsum(logit, wide, row_parts.at[ITERS, 31], weights)
    send_row(ITERS)

    def last_product(t, _):
        r = rows_at(256 * t, 256)
        partial[r, :] = jnp.dot(data_t[r, :], weights[...], preferred_element_type=F32)
        return 0

    lax.fori_loop(0, D // 256, last_product, 0)
    norms(noise_full, noise_norm)
    col_ref[...] = g_packed[...] * TO_POTENTIAL + data_norm[...] * (1.0 / D)
    wait_for(row_parts.at[ITERS, pl.ds(0, 31)], row_recv.at[ITERS])
    logsum = combine(row_parts.at[ITERS], 32)
    row_ref[...] = (math.log2(COLS * NY * NZ) - logsum) * TO_POTENTIAL + noise_norm[...] * (1.0 / D)
    scale = jnp.concatenate([jnp.exp2(top[c][:1] - logsum[c : c + 1, :]) for c in range(8)], axis=1)

    sum_a, sum_b = pl.ds(0, SUM_ZY), pl.ds(SUM_ZY, ROWS - SUM_ZY)
    scale_a, scale_b = scale[:, :SUM_ZY], scale[:, SUM_ZY:]

    def scaled(by, bz, lanes, factor):
        return partial[rows_at((by * NZ + bz) * WIDTH, WIDTH), lanes] * factor

    for dz in Z_FAR:
        to = zs[dz]
        for by in range(NY):
            partial_half[by, to, :, sum_a] = scaled(by, to, sum_a, scale_a).astype(BF16)
        remote(partial_half.at[:, to, :, sum_a], sum_zy1.at[dz - 1], a1_send, a1_recv, dp_peer(0, dz))
    for dz in Z_FAR + [0]:
        to = zs[dz]
        for dy in Y_FAR:
            by = ys[dy]
            partial_half[by, to, :, sum_b] = scaled(by, to, sum_b, scale_b).astype(BF16)
            remote(partial_half.at[by, to, :, sum_b], sum_yz1.at[dz, dy - 1], b1_send, b1_recv.at[dz], dp_peer(dy, 0))

    def sum_y(dz):
        wait_for(sum_yz1.at[dz], b1_recv.at[dz])
        total = scaled(ys[0], zs[dz], sum_b, scale_b)
        for s in range(NY - 1):
            total = total + sum_yz1[dz, s].astype(F32)
        return total

    for dz in Z_FAR:
        send_yz2[dz - 1] = sum_y(dz).astype(BF16)
        remote(send_yz2.at[dz - 1], sum_yz2.at[dz - 1], b2_send, b2_recv, dp_peer(0, dz))

    wait_for(sum_zy1, a1_recv)

    def sum_z(by):
        total = scaled(by, zs[0], sum_a, scale_a)
        for s in range(NZ - 1):
            total = total + sum_zy1[s, by].astype(F32)
        return total

    for dy in Y_FAR:
        send_zy2[dy - 1] = sum_z(ys[dy]).astype(BF16)
        remote(send_zy2.at[dy - 1], sum_zy2.at[dy - 1], a2_send, a2_recv, dp_peer(dy, 0))

    total_a = sum_z(ys[0])
    total_b = sum_y(0)
    wait_for(sum_zy2, a2_recv)
    for s in range(NY - 1):
        total_a = total_a + sum_zy2[s].astype(F32)
    targets_ref[:, sum_a] = total_a
    wait_for(sum_yz2, b2_recv)
    for s in range(NZ - 1):
        total_b = total_b + sum_yz2[s].astype(F32)
    targets_ref[:, sum_b] = total_b

    wait_for(noise_full.at[pl.ds(0, 7 * WIDTH), lanes_a], zy1_send)
    wait_for(noise_full.at[pl.ds(0, 24 * WIDTH), lanes_a], zy2_send)
    wait_for(noise_full.at[pl.ds(0, 3 * WIDTH), lanes_b], yz1_send)
    wait_for(noise_full.at[pl.ds(0, 28 * WIDTH), lanes_b], yz2_send)
    wait_for(data_full.at[:, pl.ds(0, 3 * DEPTH)], data_send)
    wait_for(data_full.at[:, pl.ds(0, 4 * DEPTH)], pair_send)
    for t in range(ITERS + 1):
        wait_for(row_parts.at[t, pl.ds(0, 31)], row_send.at[t])
    for t in range(ITERS):
        wait_for(col_parts.at[t, pl.ds(0, 7)], col_send.at[t])
    wait_for(sum_zy1, a1_send)
    wait_for(sum_zy2, a2_send)
    wait_for(sum_yz1, b1_send)
    wait_for(sum_yz2, b2_send)


def body(noise_latents, data_latents):
    dma = pltpu.SemaphoreType.DMA
    rest = ROWS - SUM_ZY
    targets, row_potential, col_potential = pl.pallas_call(
        kernel,
        out_shape=(
            jax.ShapeDtypeStruct((WIDTH, ROWS), F32),
            jax.ShapeDtypeStruct((8, 128), F32),
            jax.ShapeDtypeStruct((8, 128), F32),
        ),
        in_specs=[pl.BlockSpec(memory_space=pl.ANY)] * 2,
        out_specs=[pl.BlockSpec(memory_space=pltpu.VMEM)] * 3,
        scratch_shapes=[
            pltpu.VMEM((D, ROWS), BF16),
            pltpu.VMEM((COLS, D), BF16),
            pltpu.VMEM((D, COLS), BF16),
            pltpu.VMEM((COLS, ROWS), F32),
            pltpu.VMEM((COLS, ROWS), BF16),
            pltpu.VMEM((D, ROWS), F32),
            pltpu.VMEM((NY, NZ, WIDTH, ROWS), BF16),
            pltpu.VMEM((COLS, 128), F32),
            pltpu.VMEM((8, 128), F32),
            pltpu.VMEM((8, 128), F32),
            pltpu.VMEM((8, 128), F32),
            pltpu.VMEM((8, 128), F32),
            pltpu.VMEM((ITERS + 1, 32, 8, 128), F32),
            pltpu.VMEM((ITERS, 8, 8, 128), F32),
            pltpu.VMEM((NZ, NY - 1, WIDTH, rest), BF16),
            pltpu.VMEM((NZ - 1, WIDTH, rest), BF16),
            pltpu.VMEM((NZ - 1, NY, WIDTH, SUM_ZY), BF16),
            pltpu.VMEM((NY - 1, WIDTH, SUM_ZY), BF16),
            pltpu.VMEM((NZ - 1, WIDTH, rest), BF16),
            pltpu.VMEM((NY - 1, WIDTH, SUM_ZY), BF16),
            dma((2,)),
            dma, dma((NX,)), dma, dma((NX,)),
            dma, dma((NZ,)), dma, dma,
            dma, dma((NY,)), dma, dma,
            dma((ITERS + 1,)), dma((ITERS + 1,)), dma((ITERS,)), dma((ITERS,)),
            dma, dma, dma, dma,
            dma, dma((NZ,)), dma, dma,
        ],
        compiler_params=pltpu.CompilerParams(
            collective_id=0, has_side_effects=True, vmem_limit_bytes=48 << 20
        ),
    )(noise_latents.T, data_latents)
    return targets.T, row_potential.reshape(ROWS), col_potential.reshape(COLS)


def solution(mesh):
    return jax.shard_map(
        body,
        mesh=mesh,
        in_specs=(P("noise", "dp"), P("dp", "noise")),
        out_specs=(P("noise", "dp"), P("noise"), P("dp")),
        check_vma=False,
    )
```
